256 devices in a mesh: dp: 32 (over x, y, z_lo), tensor: 8 (over z_hi, core).
Axes of the slice: x: 4, y: 4, z: 8 (z_hi: 4, z_lo: 2; z = z_hi * 2 + z_lo), core: 2. Of those that a mesh axis runs over, the one named last changes fastest.
Arguments:
- latent_x: bfloat16 [1280, 32768], P('tensor', 'dp'), parts along dimension 1, may hold values from -6 to 6
- control_h: bfloat16 [1280, 32768], P('tensor', 'dp'), parts along dimension 1, may hold values from -6 to 6
- tile_mask: int32 [32, 8, 8], P('dp'), parts along dimension 0, may hold values 0 or 1
- timestep: int32 [32], P('dp'), parts along dimension 0, may hold values from 0 to 999
- time_weight: bfloat16 [320, 1280], P(None, 'tensor'), may hold values from -0.5 to 0.5
- norm_gain: float32 [3, 1280], P(None, 'tensor'), may hold values from 0.5 to 1.5
- norm_bias: float32 [3, 1280], P(None, 'tensor'), may hold values from -3 to 3
- unet_conv_in: bfloat16 [9, 1280, 1280], P(None, 'tensor'), may hold values from -0.0546875 to 0.0546875
- unet_conv_out: bfloat16 [9, 1280, 1280], P(None, 'tensor'), may hold values from -0.0546875 to 0.0546875
- control_conv: bfloat16 [9, 1280, 1280], P(None, 'tensor'), may hold values from -0.0546875 to 0.0546875
- unet_temb: bfloat16 [1280, 1280], P('tensor'), may hold values from -0.15625 to 0.15625
- control_temb: bfloat16 [1280, 1280], P('tensor'), may hold values from -0.15625 to 0.15625
- zero_conv: bfloat16 [1280, 1280], P('tensor'), may hold values from -0.15625 to 0.15625
Outputs:
- mixed: bfloat16 [1280, 32768], P('tensor', 'dp'), parts along dimension 1
The draws below stay inside these ranges and needn't reach their ends.
There are 32 independent parts, one for each index of `dp`. The reference program is written for one: setup_inputs(seed, part) draws one part's arguments, and reference() takes and returns one part's arrays. A program takes and returns all parts, laid end to end along the dimension named above; an argument that names none is the same for every part. Nothing has to cross between parts.
All inputs are finite; a program needn't handle non-finite values.
Results may differ from the reference program's by a relative error of at most 0.014.
Values may be sent and summed in bfloat16 or wider, within the bound.
A program may use at most 128 MiB of HBM per device.

```python
import math
import jax
import jax.numpy as jnp
from jax import lax

C = 1280
GROUPS = 32
FREQ = 320
S = 32
TILE = 4
VIEWS = 1
P_SIZE = 1024


def plant(drawn, stream_key, low, largest):
    spot = [jax.random.randint(jax.random.fold_in(stream_key, axis), (), 0, length) for axis, length in enumerate(drawn.shape)]
    widest = drawn.shape.index(max(drawn.shape))
    next_to = spot[:widest] + [(spot[widest] + 1) % drawn.shape[widest]] + spot[widest + 1:]
    return drawn.at[tuple(spot)].set(low).at[tuple(next_to)].set(largest)


def block_levels(stream_key, extent, split, smallest, largest):
    def one(dim, shards_of):
        steps = jax.random.uniform(jax.random.fold_in(jax.random.fold_in(stream_key, 6), dim), (shards_of,), jnp.float32, smallest / len(split), largest / len(split))
        return jnp.repeat(jnp.exp(steps), extent[dim] // shards_of).reshape((-1,) + (1,) * (len(extent) - dim - 1))

    factor_of = one(*split[0])
    for cut in split[1:]:
        factor_of = factor_of * one(*cut)
    return factor_of


def bell_draw(stream_key, dims, width, most, cuts=(), kind=jnp.bfloat16):
    values = jax.random.normal(stream_key, dims, jnp.float32) * width
    if len(cuts) > 0:
        values = block_levels(stream_key, dims, cuts, -0.22, 0.18) * values
    return jnp.clip(values, min=-most, max=most).astype(kind)


def setup_inputs(seed: int = 0, part: int = 0) -> dict:
    splits = jax.random.split(jax.random.key(seed), 14)
    part_keys = jax.random.split(jax.random.fold_in(splits[13], part), 14)
    return {
        "latent_x": bell_draw(part_keys[0], (C, P_SIZE), 1.0, 6.0, ((0, 8),)),
        "control_h": bell_draw(part_keys[1], (C, P_SIZE), 1.0, 6.0, ((0, 8),)),
        "tile_mask": plant((jax.random.randint(part_keys[2], (VIEWS, S // TILE, S // TILE), 0, 2) < 1).astype(jnp.int32), jax.random.fold_in(part_keys[2], 1), 0, 1),
        "timestep": jax.random.randint(part_keys[3], (1,), 0, 1000).astype(jnp.int32),
        "time_weight": bell_draw(splits[4], (FREQ, C), (FREQ // 2) ** -0.5, 0.5, ((1, 8),)),
        "norm_gain": jnp.clip(1.0 + 0.1 * jax.random.normal(splits[5], (3, C), jnp.float32), 0.5, 1.5),
        "norm_bias": bell_draw(splits[6], (3, C), 0.5, 3.0, ((1, 8),), jnp.float32),
        "unet_conv_in": bell_draw(splits[7], (9, C, C), (9 * C) ** -0.5, 0.0546875, ((1, 8),)),
        "unet_conv_out": bell_draw(splits[8], (9, C, C), (9 * C) ** -0.5, 0.0546875, ((1, 8),)),
        "control_conv": bell_draw(splits[9], (9, C, C), (9 * C) ** -0.5, 0.0546875, ((1, 8),)),
        "unet_temb": bell_draw(splits[10], (C, C), C ** -0.5, 0.15625, ((0, 8),)),
        "control_temb": bell_draw(splits[11], (C, C), C ** -0.5, 0.15625, ((0, 8),)),
        "zero_conv": bell_draw(splits[12], (C, C), C ** -0.5, 0.15625, ((0, 8),)),
    }


def timestep_features(timestep):
    half_width = FREQ // 2
    rates = jnp.exp(-math.log(10000.0) * jnp.arange(half_width, dtype=jnp.float32) / half_width)
    angles = timestep.astype(jnp.float32)[0] * rates
    return jnp.concatenate([jnp.cos(angles), jnp.sin(angles)])

def norm_silu(inputs, scales, shifts):
    rows_count = inputs.shape[0]
    group_size = C // GROUPS
    grouped = inputs.astype(jnp.float32).reshape(rows_count // group_size, group_size, VIEWS, S * S)
    average = lax.optimization_barrier(jnp.mean(grouped, axis=(1, 3), keepdims=True))
    centred = grouped - average
    variance = lax.optimization_barrier(jnp.mean(centred * centred, axis=(1, 3), keepdims=True))
    normed = (centred * lax.rsqrt(variance + 1e-05)).reshape(rows_count, VIEWS * S * S)
    return jax.nn.silu(normed * scales[:, None] + shifts[:, None]).astype(jnp.bfloat16)

def shifted_copies(inputs):
    rows_count = inputs.shape[0]
    picture = inputs.reshape(rows_count, VIEWS, S, S)
    padded = jnp.pad(picture, ((0, 0), (0, 0), (1, 1), (1, 1)))
    copies = []
    for row_step in range(3):
        for col_step in range(3):
            copies.append(padded[:, :, row_step:row_step + S, col_step:col_step + S].reshape(rows_count, VIEWS * S * S))
    return copies

def convolve(inputs, weights, flipped):
    copies = shifted_copies(inputs)
    out_rows = weights.shape[2] if flipped else weights.shape[1]
    result = jnp.zeros((out_rows, inputs.shape[1]), jnp.float32)
    for place in range(9):
        tap = weights[place].T if flipped else weights[place]
        result = result + jnp.dot(tap, copies[place], preferred_element_type=jnp.float32)
    return result

def expand_mask(tile_mask):
    blocks = tile_mask.astype(jnp.float32)[:, :, None, :, None]
    spread_mask = jnp.broadcast_to(blocks, (VIEWS, S // TILE, TILE, S // TILE, TILE))
    return spread_mask.reshape(VIEWS * S * S)

def reference(latent_x, control_h, tile_mask, timestep, time_weight, norm_gain, norm_bias, unet_conv_in, unet_conv_out, control_conv, unet_temb, control_temb, zero_conv):
    time_vector = jax.nn.silu(jnp.dot(timestep_features(timestep), time_weight.astype(jnp.float32), precision=lax.Precision.HIGHEST))
    unet_shift = jnp.dot(unet_temb.astype(jnp.float32), time_vector, precision=lax.Precision.HIGHEST)
    control_shift = jnp.dot(control_temb.astype(jnp.float32), time_vector, precision=lax.Precision.HIGHEST)
    first = norm_silu(latent_x, norm_gain[0], norm_bias[0])
    hidden = (convolve(first, unet_conv_in, False) + unet_shift[:, None]).astype(jnp.bfloat16)
    hidden = lax.optimization_barrier(hidden)
    second = norm_silu(hidden, norm_gain[1], norm_bias[1])
    control_act = norm_silu(control_h, norm_gain[2], norm_bias[2])
    control_state = (control_h.astype(jnp.float32) + convolve(control_act, control_conv, True) + control_shift[:, None]).astype(jnp.bfloat16)
    gate_row = expand_mask(tile_mask)
    residual = jnp.dot(zero_conv.T, control_state, preferred_element_type=jnp.float32) * gate_row[None, :]
    mixed = latent_x.astype(jnp.float32) + convolve(second, unet_conv_out, True) + residual
    return mixed.astype(jnp.bfloat16)
```

```python
import functools
import math

import jax
import jax.numpy as jnp
from jax import lax
from jax.experimental import pallas as pl
from jax.experimental.pallas import tpu as pltpu
from jax.sharding import PartitionSpec as P

F32 = jnp.float32
BF16 = jnp.bfloat16
MESH = pl.DeviceIdType.MESH

C = 1280
S = 32
CELLS = S * S
FREQ = 320
SHARDS = 8
CH = C // SHARDS
HALF = CH // 2
GROUP = 40
TAPS = 9
KPAD = 1536
NB = 256
NSTEPS = CELLS // NB


def aligned(value, multiple):
    return pl.multiple_of(value, multiple)


def silu(v):
    return 0.5 * v * (1.0 + jnp.tanh(0.5 * v))


def dot(a, b):
    return jnp.dot(a, b, preferred_element_type=F32)


def cell_masks(rows):
    lane = lax.broadcasted_iota(jnp.int32, (rows, CELLS), 1)
    col = lane % S
    left = (col >= 1).astype(F32)
    right = (col <= S - 2).astype(F32)
    up = (lane >= S).astype(F32)
    down = (lane < CELLS - S).astype(F32)
    return left, right, up, down


def group_norm_silu(xf, gain, bias, group):
    rows = pl.ds(group * GROUP, GROUP)
    v = xf[rows, :]
    mean = jnp.sum(v, keepdims=True) * (1.0 / (GROUP * CELLS))
    centred = v - mean
    var = jnp.sum(centred * centred, keepdims=True) * (1.0 / (GROUP * CELLS))
    normed = centred * lax.rsqrt(var + 1e-5)
    xf[rows, :] = silu(normed * gain + bias)


def shifted_stack(xf, stack):
    def body(i, carry):
        r = aligned(i * 16, 16)
        left, right, up, down = cell_masks(16)
        v = xf[pl.ds(r, 16), :]
        columns = (
            pltpu.roll(v, 1, 1) * left,
            v,
            pltpu.roll(v, CELLS - 1, 1) * right,
        )
        for dx, w in enumerate(columns):
            stack[pl.ds(aligned((0 + dx) * CH + r, 16), 16), :] = (
                pltpu.roll(w, S, 1) * up
            ).astype(BF16)
            stack[pl.ds(aligned((3 + dx) * CH + r, 16), 16), :] = w.astype(BF16)
            stack[pl.ds(aligned((6 + dx) * CH + r, 16), 16), :] = (
                pltpu.roll(w, CELLS - S, 1) * down
            ).astype(BF16)
        return carry

    lax.fori_loop(0, CH // 16, body, 0)


def transpose_into(dst, src, out_blocks, in_rows):
    def body(i, carry):
        m = aligned(i * 128, 128)
        dst[pl.ds(m, 128), :] = src[:, pl.ds(m, 128)].T
        return carry

    lax.fori_loop(0, out_blocks, body, 0)


def kernel(
    step_ref,
    mask_ref,
    gain_ref,
    bias_ref,
    latent_hbm,
    control_hbm,
    time_hbm,
    win_hbm,
    wout_hbm,
    cw_hbm,
    utemb_hbm,
    ctemb_hbm,
    zero_hbm,
    out_hbm,
    latent,
    control,
    time_w,
    win,
    wraw,
    craw,
    wt,
    ct,
    utemb,
    ctemb,
    zraw,
    zt,
    gathered,
    taps_sum,
    stack,
    wide,
    state,
    xf,
    norm_in,
    norm_cols,
    shifts,
    gate,
    tv_mine,
    tv_all,
    tv_row,
    sib_send,
    sib_recv,
    far_send,
    far_recv,
    near_send,
    near_recv,
    out_buf,
    load_sem,
    zload_sem,
    out_sem,
    ag_send,
    ag_recv,
    d2d_send,
    d2d_recv,
    tv_send,
    tv_recv,
    sib_ssem,
    sib_rsem,
    rs_send,
    rs_recv,
):
    tensor = lax.axis_index("tensor")
    k = tensor // 2
    c = tensor % 2
    k_up = (k + 1) % 4
    k_down = (k + 3) % 4
    k_far = (k + 2) % 4
    sib = {"tensor": k * 2 + (1 - c)}
    up = {"tensor": k_up * 2 + c}
    down = {"tensor": k_down * 2 + c}

    loads = {}
    for i, (name, src, dst) in enumerate(
        (
            ("latent", latent_hbm, latent),
            ("time", time_hbm, time_w),
            ("control", control_hbm, control),
            ("ctemb", ctemb_hbm, ctemb),
            ("utemb", utemb_hbm, utemb),
            ("craw", cw_hbm, craw.at[pl.ds(0, TAPS * CH), :]),
            ("win", win_hbm, win),
            ("wraw", wout_hbm, wraw.at[pl.ds(0, TAPS * CH), :]),
        )
    ):
        loads[name] = pltpu.make_async_copy(src, dst, load_sem.at[i])
        loads[name].start()
    zloads = []
    for d in range(4):
        copy = pltpu.make_async_copy(
            zero_hbm.at[pl.ds(aligned((2 * d + c) * CH, 32), CH), :],
            zraw.at[pl.ds(d * CH, CH), :],
            zload_sem.at[d],
        )
        copy.start()
        zloads.append(copy)

    barrier = pltpu.get_barrier_semaphore()
    for step in range(1, SHARDS):
        pl.semaphore_signal(
            barrier, inc=1, device_id={"tensor": (tensor + step) % SHARDS}, device_id_type=MESH
        )

    norm_in[...] = jnp.zeros_like(norm_in)
    norm_in[0:3, 0:CH] = gain_ref[...]
    norm_in[3:6, 0:CH] = bias_ref[...]
    norm_cols[...] = norm_in[...].T

    loads["latent"].wait()

    def widen(src):
        def body(i, carry):
            r = aligned(i * 16, 16)
            xf[pl.ds(r, 16), :] = src[pl.ds(r, 16), :].astype(F32)
            return carry

        lax.fori_loop(0, CH // 16, body, 0)

    def slot_rows(shard, half):
        return pl.ds(aligned(32 * (shard % 4) + half * HALF, 16), HALF)

    def norm_half(which, half):
        for group in (2 * half, 2 * half + 1):
            rows = slice(group * GROUP, (group + 1) * GROUP)
            group_norm_silu(
                xf, norm_cols[rows, which : which + 1], norm_cols[rows, 3 + which : 4 + which], group
            )

    def piece(shard, half):
        return gathered.at[shard, slot_rows(shard, half), :]

    def remote(ref, send, recv, target, dst=None):
        return pltpu.make_async_remote_copy(
            src_ref=ref,
            dst_ref=ref if dst is None else dst,
            send_sem=send,
            recv_sem=recv,
            device_id=target,
            device_id_type=MESH,
        )

    def ag_copy(shard, half, slot, target):
        return remote(piece(shard, half), ag_send.at[slot], ag_recv.at[slot], target)

    def d2d_copy(shard, half, which):
        slot = which * 2 + half
        return remote(piece(shard, half), d2d_send.at[slot], d2d_recv.at[slot], sib)

    widen(latent)
    started = []

    def start(copy):
        copy.start()
        started.append(copy)

    for half in (0, 1):
        norm_half(0, half)
        for i in range(HALF // 16):
            r = half * HALF + i * 16
            gathered[tensor, pl.ds(aligned(32 * (tensor % 4) + r, 16), 16), :] = xf[
                r : r + 16, :
            ].astype(BF16)
        if half == 0:
            pl.semaphore_wait(barrier, SHARDS - 1)
            start(ag_copy(tensor, 0, 0, up))
            start(d2d_copy(tensor, 0, 0))
        else:
            start(ag_copy(tensor, 1, 2, down))
            start(ag_copy(tensor, 1, 1, up))
            start(ag_copy(tensor, 0, 3, down))
            start(d2d_copy(tensor, 1, 0))

    loads["time"].wait()
    index = lax.broadcasted_iota(jnp.int32, (8, NB), 1).astype(F32)
    rates = jnp.exp(-math.log(10000.0) * index / (FREQ // 2))
    angles = step_ref[0].astype(F32) * rates
    local = jnp.zeros((8, CH), F32)
    for part, feats in enumerate((jnp.cos(angles), jnp.sin(angles))):
        weights = time_w[part * CH : (part + 1) * CH, :]
        rest = feats[:, 0:CH]
        for _ in range(3):
            top = rest.astype(BF16)
            local = local + dot(top, weights)
            rest = rest - top.astype(F32)
    tv_mine[...] = jnp.zeros_like(tv_mine)
    tv_mine[:, 0:CH] = silu(local)
    tv_mine[...] = pltpu.roll(tv_mine[...], 32 * (tensor % 4), 1)
    for step in range(1, SHARDS):
        start(
            remote(
                tv_mine,
                tv_send.at[step],
                tv_recv.at[step],
                {"tensor": (tensor + step) % SHARDS},
                tv_all.at[step],
            )
        )

    for shard in range(SHARDS):
        low = 32 * (shard % 4)
        if low:
            gathered[shard, 0:low, :] = jnp.zeros((low, CELLS), BF16)
        if low + CH < NB:
            gathered[shard, low + CH : NB, :] = jnp.zeros((NB - low - CH, CELLS), BF16)
    pad = KPAD - TAPS * CH
    stack[TAPS * CH : KPAD, :] = jnp.zeros((pad, CELLS), BF16)
    wraw[TAPS * CH : KPAD, :] = jnp.zeros((pad, C), BF16)
    craw[TAPS * CH : KPAD, :] = jnp.zeros((pad, C), BF16)

    tile = lax.broadcasted_iota(jnp.int32, (8, 128), 0)
    lane = lax.broadcasted_iota(jnp.int32, (8, 128), 1)
    spread = (lane % S // 4 == tile).astype(BF16)
    by_row = dot(mask_ref[0].astype(F32).astype(BF16), spread)
    for row in range(8):
        gate[:, row * 128 : (row + 1) * 128] = jnp.broadcast_to(by_row[row : row + 1, :], (8, 128))

    loads["control"].wait()
    widen(control)
    norm_half(2, 0)
    norm_half(2, 1)
    shifted_stack(xf, stack)
    loads["craw"].wait()
    transpose_into(ct, craw, C // 128, KPAD)

    def control_body(n, carry):
        lanes = pl.ds(aligned(n * NB, NB), NB)
        wide[:, lanes] = dot(ct[...], stack[:, lanes])
        return carry

    lax.fori_loop(0, NSTEPS, control_body, 0)

    def window(shard):
        return pl.ds(aligned(128 * ((5 * shard) // 4), 128), NB)

    def conv_in(chip, first_time):
        def body(n, carry):
            lanes = pl.ds(aligned(n * NB, NB), NB)
            total = dot(win[:, window(2 * chip)], gathered[2 * chip, :, lanes])
            total = total + dot(win[:, window(2 * chip + 1)], gathered[2 * chip + 1, :, lanes])
            if first_time:
                taps_sum[:, lanes] = total
            else:
                taps_sum[:, lanes] = taps_sum[:, lanes] + total
            return carry

        lax.fori_loop(0, NSTEPS, body, 0)

    mate_k = lambda chip: chip * 2 + c
    other_k = lambda chip: chip * 2 + (1 - c)
    ag_copy(mate_k(k_down), 0, 0, up).wait_recv()
    start(ag_copy(mate_k(k_down), 0, 4, up))
    start(d2d_copy(mate_k(k_down), 0, 1))
    ag_copy(mate_k(k_up), 1, 2, down).wait_recv()
    start(ag_copy(mate_k(k_up), 1, 5, down))
    start(d2d_copy(mate_k(k_up), 1, 2))

    tv_row[...] = jnp.zeros_like(tv_row)
    tv_row[:, window(tensor)] = tv_row[:, window(tensor)] + tv_mine[...]
    for step in range(1, SHARDS):
        remote(tv_mine, tv_send.at[step], tv_recv.at[step], sib, tv_all.at[step]).wait_recv()
        owner = (tensor + SHARDS - step) % SHARDS
        tv_row[:, window(owner)] = tv_row[:, window(owner)] + tv_all[step]
    loads["ctemb"].wait()
    loads["utemb"].wait()
    for which, table in enumerate((utemb, ctemb)):

        def temb_body(i, carry):
            r = aligned(i * 16, 16)
            product = table[pl.ds(r, 16), :].astype(F32) * tv_row[0:1, :]
            shifts[which, pl.ds(r, 16), :] = jnp.broadcast_to(
                jnp.sum(product, axis=1, keepdims=True), (16, 128)
            )
            return carry

        lax.fori_loop(0, CH // 16, temb_body, 0)

    own = pl.ds(aligned(tensor * CH, 32), CH)
    wide[own, :] = wide[own, :] + (control[...].astype(F32) + shifts[1, :, 0:1])
    for d in range(4):
        theirs = pl.ds(aligned((2 * d + 1 - c) * CH, 32), CH)
        sib_send[d] = wide[theirs, :].astype(BF16)
        start(remote(sib_send.at[d], sib_ssem.at[d], sib_rsem.at[d], sib, sib_recv.at[d]))

    loads["win"].wait()
    d2d_copy(tensor, 0, 0).wait_recv()
    d2d_copy(tensor, 1, 0).wait_recv()
    conv_in(k, True)

    for copy in zloads:
        copy.wait()
    transpose_into(zt, zraw, C // 128, 4 * CH)
    for d in range(4):
        mine = pl.ds(aligned((2 * d + c) * CH, 32), CH)
        remote(sib_send.at[d], sib_ssem.at[d], sib_rsem.at[d], sib, sib_recv.at[d]).wait_recv()
        state[pl.ds(d * CH, CH), :] = (wide[mine, :] + sib_recv[d].astype(F32)).astype(BF16)

    def residual_body(n, carry):
        lanes = pl.ds(aligned(n * NB, NB), NB)
        wide[:, lanes] = dot(zt[...], state[:, lanes]) * gate[0:1, lanes]
        return carry

    lax.fori_loop(0, NSTEPS, residual_body, 0)

    loads["wraw"].wait()
    transpose_into(wt, wraw, C // 128, KPAD)

    ag_copy(mate_k(k_down), 1, 1, up).wait_recv()
    start(d2d_copy(mate_k(k_down), 1, 1))
    ag_copy(mate_k(k_up), 0, 3, down).wait_recv()
    start(d2d_copy(mate_k(k_up), 0, 2))
    d2d_copy(other_k(k_down), 0, 1).wait_recv()
    d2d_copy(other_k(k_down), 1, 1).wait_recv()
    conv_in(k_down, False)
    d2d_copy(other_k(k_up), 1, 2).wait_recv()
    d2d_copy(other_k(k_up), 0, 2).wait_recv()
    conv_in(k_up, False)
    ag_copy(mate_k(k_far), 0, 4, up).wait_recv()
    start(d2d_copy(mate_k(k_far), 0, 3))
    ag_copy(mate_k(k_far), 1, 5, down).wait_recv()
    start(d2d_copy(mate_k(k_far), 1, 3))
    d2d_copy(other_k(k_far), 0, 3).wait_recv()
    d2d_copy(other_k(k_far), 1, 3).wait_recv()
    conv_in(k_far, False)

    def hidden_body(i, carry):
        r = aligned(i * 8, 8)
        left, right, above, below = cell_masks(8)

        def tap(t):
            return taps_sum[pl.ds(aligned(t * CH + r, 8), 8), :]

        def row(dy):
            return (
                pltpu.roll(tap(3 * dy), 1, 1) * left
                + tap(3 * dy + 1)
                + pltpu.roll(tap(3 * dy + 2), CELLS - 1, 1) * right
            )

        total = pltpu.roll(row(0), S, 1) * above + row(1)
        total = total + pltpu.roll(row(2), CELLS - S, 1) * below
        total = total + shifts[0, pl.ds(r, 8), 0:1]
        xf[pl.ds(r, 8), :] = total.astype(BF16).astype(F32)
        return carry

    lax.fori_loop(0, CH // 8, hidden_body, 0)
    norm_half(1, 0)
    norm_half(1, 1)
    shifted_stack(xf, stack)

    for copy in started:
        copy.wait_send()

    def conv_out(chip):
        rows = pl.ds(aligned(chip * 2 * CH, 64), 2 * CH)

        def body(n, carry):
            lanes = pl.ds(aligned(n * NB, NB), NB)
            wide[rows, lanes] = wide[rows, lanes] + dot(wt[rows, :], stack[:, lanes])
            return carry

        lax.fori_loop(0, NSTEPS, body, 0)

    def to_sibling(slot, chip):
        theirs = pl.ds(aligned((2 * chip + 1 - c) * CH, 32), CH)
        sib_send[slot] = wide[theirs, :].astype(BF16)
        remote(
            sib_send.at[slot], sib_ssem.at[4 + slot], sib_rsem.at[4 + slot], sib, sib_recv.at[4 + slot]
        ).start()

    def from_sibling(slot):
        remote(
            sib_send.at[slot], sib_ssem.at[4 + slot], sib_rsem.at[4 + slot], sib, sib_recv.at[4 + slot]
        ).wait_recv()

    def own_sum(slot, chip, half):
        mine = pl.ds(aligned((2 * chip + c) * CH + half * HALF, 16), HALF)
        part = slice(half * HALF, (half + 1) * HALF)
        return wide[mine, :] + sib_recv[4 + slot, part, :].astype(F32)

    def far_copy(half):
        return remote(
            far_send.at[half], rs_send.at[half], rs_recv.at[half], (up, down)[half], far_recv.at[half]
        )

    def near_copy(way, half):
        slot = 2 + 2 * way + half
        return remote(
            near_send.at[way, half],
            rs_send.at[slot],
            rs_recv.at[slot],
            (up, down)[way],
            near_recv.at[way, half],
        )

    conv_out(k_far)
    to_sibling(0, k_far)
    conv_out(k_up)
    to_sibling(1, k_up)
    from_sibling(0)
    for half in (0, 1):
        far_send[half] = own_sum(0, k_far, half).astype(BF16)
        far_copy(half).start()
    conv_out(k_down)
    to_sibling(2, k_down)
    from_sibling(1)
    near_send[0, 1] = own_sum(1, k_up, 1).astype(BF16)
    near_copy(0, 1).start()
    conv_out(k)
    to_sibling(3, k)
    from_sibling(2)
    near_send[1, 0] = own_sum(2, k_down, 0).astype(BF16)
    near_copy(1, 0).start()
    from_sibling(3)
    far_copy(0).wait_recv()
    near_send[0, 0] = (own_sum(1, k_up, 0) + far_recv[0].astype(F32)).astype(BF16)
    near_copy(0, 0).start()
    far_copy(1).wait_recv()
    near_send[1, 1] = (own_sum(2, k_down, 1) + far_recv[1].astype(F32)).astype(BF16)
    near_copy(1, 1).start()
    for half in (0, 1):
        part = slice(half * HALF, (half + 1) * HALF)
        xf[part, :] = own_sum(3, k, half) + latent[part, :].astype(F32)
    near_copy(0, 1).wait_recv()
    xf[HALF:, :] = xf[HALF:, :] + near_recv[0, 1].astype(F32)
    near_copy(1, 0).wait_recv()
    xf[:HALF, :] = xf[:HALF, :] + near_recv[1, 0].astype(F32)
    near_copy(0, 0).wait_recv()
    out_buf[:HALF, :] = (xf[:HALF, :] + near_recv[0, 0].astype(F32)).astype(BF16)
    store0 = pltpu.make_async_copy(
        out_buf.at[pl.ds(0, HALF), :], out_hbm.at[pl.ds(0, HALF), :], out_sem.at[0]
    )
    store0.start()
    near_copy(1, 1).wait_recv()
    out_buf[HALF:, :] = (xf[HALF:, :] + near_recv[1, 1].astype(F32)).astype(BF16)
    store1 = pltpu.make_async_copy(
        out_buf.at[pl.ds(HALF, HALF), :], out_hbm.at[pl.ds(HALF, HALF), :], out_sem.at[1]
    )
    store1.start()
    for slot in range(4):
        remote(
            sib_send.at[slot], sib_ssem.at[4 + slot], sib_rsem.at[4 + slot], sib, sib_recv.at[4 + slot]
        ).wait_send()
    for half in (0, 1):
        far_copy(half).wait_send()
        near_copy(0, half).wait_send()
        near_copy(1, half).wait_send()
    store0.wait()
    store1.wait()


def local(
    latent_x,
    control_h,
    tile_mask,
    timestep,
    time_weight,
    norm_gain,
    norm_bias,
    unet_conv_in,
    unet_conv_out,
    control_conv,
    unet_temb,
    control_temb,
    zero_conv,
):
    zero_all = lax.all_gather(zero_conv, "tensor", axis=0, tiled=True)
    flat = lambda w: w.reshape(TAPS * CH, C)
    smem = pl.BlockSpec(memory_space=pltpu.SMEM)
    vmem = pl.BlockSpec(memory_space=pltpu.VMEM)
    hbm = pl.BlockSpec(memory_space=pl.ANY)
    dma = pltpu.SemaphoreType.DMA
    return pl.pallas_call(
        kernel,
        out_shape=jax.ShapeDtypeStruct((CH, CELLS), BF16),
        in_specs=[smem, vmem, vmem, vmem] + [hbm] * 9,
        out_specs=hbm,
        scratch_shapes=[
            pltpu.VMEM((CH, CELLS), BF16),
            pltpu.VMEM((CH, CELLS), BF16),
            pltpu.VMEM((FREQ, CH), BF16),
            pltpu.VMEM((TAPS * CH, C), BF16),
            pltpu.VMEM((KPAD, C), BF16),
            pltpu.VMEM((KPAD, C), BF16),
            pltpu.VMEM((C, KPAD), BF16),
            pltpu.VMEM((C, KPAD), BF16),
            pltpu.VMEM((CH, C), BF16),
            pltpu.VMEM((CH, C), BF16),
            pltpu.VMEM((4 * CH, C), BF16),
            pltpu.VMEM((C, 4 * CH), BF16),
            pltpu.VMEM((SHARDS, NB, CELLS), BF16),
            pltpu.VMEM((TAPS * CH, CELLS), F32),
            pltpu.VMEM((KPAD, CELLS), BF16),
            pltpu.VMEM((C, CELLS), F32),
            pltpu.VMEM((4 * CH, CELLS), BF16),
            pltpu.VMEM((CH, CELLS), F32),
            pltpu.VMEM((8, 256), F32),
            pltpu.VMEM((256, 8), F32),
            pltpu.VMEM((2, CH, 128), F32),
            pltpu.VMEM((8, CELLS), F32),
            pltpu.VMEM((8, NB), F32),
            pltpu.VMEM((SHARDS, 8, NB), F32),
            pltpu.VMEM((8, C), F32),
            pltpu.VMEM((4, CH, CELLS), BF16),
            pltpu.VMEM((8, CH, CELLS), BF16),
            pltpu.VMEM((2, HALF, CELLS), BF16),
            pltpu.VMEM((2, HALF, CELLS), BF16),
            pltpu.VMEM((2, 2, HALF, CELLS), BF16),
            pltpu.VMEM((2, 2, HALF, CELLS), BF16),
            pltpu.VMEM((CH, CELLS), BF16),
            dma((8,)),
            dma((4,)),
            dma((2,)),
            dma((6,)),
            dma((6,)),
            dma((8,)),
            dma((8,)),
            dma((8,)),
            dma((8,)),
            dma((8,)),
            dma((8,)),
            dma((6,)),
            dma((6,)),
        ],
        compiler_params=pltpu.CompilerParams(
            collective_id=0, has_side_effects=True, vmem_limit_bytes=62 * 1024 * 1024
        ),
        name="block",
    )(
        timestep,
        tile_mask,
        norm_gain,
        norm_bias,
        latent_x,
        control_h,
        time_weight,
        flat(unet_conv_in),
        flat(unet_conv_out),
        flat(control_conv),
        unet_temb,
        control_temb,
        zero_all,
    )


def solution(mesh):
    placed = (
        P("tensor", "dp"),
        P("tensor", "dp"),
        P("dp", None, None),
        P("dp"),
        P(None, "tensor"),
        P(None, "tensor"),
        P(None, "tensor"),
        P(None, "tensor", None),
        P(None, "tensor", None),
        P(None, "tensor", None),
        P("tensor", None),
        P("tensor", None),
        P("tensor", None),
    )
    return jax.shard_map(
        local, mesh=mesh, in_specs=placed, out_specs=P("tensor", "dp"), check_vma=False
    )
```

```python
import functools
import math

import jax
import jax.numpy as jnp
from jax import lax
from jax.experimental import pallas as pl
from jax.experimental.pallas import tpu as pltpu
from jax.sharding import PartitionSpec as P

F32 = jnp.float32
BF16 = jnp.bfloat16
MESH = pl.DeviceIdType.MESH

C = 1280
S = 32
CELLS = S * S
FREQ = 320
SHARDS = 8
CH = C // SHARDS
HALF = CH // 2
GROUP = 40
TAPS = 9
KPAD = 1536
NB = 256
NSTEPS = CELLS // NB


def aligned(value, multiple):
    return pl.multiple_of(value, multiple)


def silu(v):
    return 0.5 * v * (1.0 + jnp.tanh(0.5 * v))


def dot(a, b):
    return jnp.dot(a, b, preferred_element_type=F32)


def fill_masks(masks):
    lane = lax.broadcasted_iota(jnp.int32, (8, CELLS), 1)
    col = lane % S
    masks[0] = (col >= 1).astype(F32)
    masks[1] = (col <= S - 2).astype(F32)
    masks[2] = (lane >= S).astype(F32)
    masks[3] = (lane < CELLS - S).astype(F32)


def group_norm_silu(xf, gain, bias, group):
    rows = pl.ds(group * GROUP, GROUP)
    v = xf[rows, :]
    mean = jnp.sum(v, keepdims=True) * (1.0 / (GROUP * CELLS))
    centred = v - mean
    var = jnp.sum(centred * centred, keepdims=True) * (1.0 / (GROUP * CELLS))
    normed = centred * lax.rsqrt(var + 1e-5)
    xf[rows, :] = silu(normed * gain + bias)


def shifted_stack(xf, stack, masks):
    rows = 32
    blocks = CELLS // 128

    def body(i, carry):
        r = aligned(i * rows, rows)
        left = jnp.concatenate([masks[0, :, 0:128]] * (rows // 8), 0)
        right = jnp.concatenate([masks[1, :, 0:128]] * (rows // 8), 0)
        lane = lax.broadcasted_iota(jnp.int32, (rows, 128), 1)
        zero = jnp.zeros((rows, 128), F32)
        v = [xf[pl.ds(r, rows), b * 128 : (b + 1) * 128] for b in range(blocks)]
        columns = (
            [pltpu.roll(x, 1, 1) * left for x in v],
            v,
            [pltpu.roll(x, 127, 1) * right for x in v],
        )
        for dx, w in enumerate(columns):
            above = [pltpu.roll(x, S, 1) for x in w] + [zero]
            below = [pltpu.roll(x, 128 - S, 1) for x in w] + [zero]
            for b in range(blocks):
                lanes = slice(b * 128, (b + 1) * 128)
                for dy, value in (
                    (0, jnp.where(lane < S, above[b - 1], above[b])),
                    (1, w[b]),
                    (2, jnp.where(lane >= 128 - S, below[b + 1], below[b])),
                ):
                    stack[pl.ds(aligned((3 * dy + dx) * CH + r, rows), rows), lanes] = value.astype(BF16)
        return carry

    lax.fori_loop(0, CH // rows, body, 0)


def transpose_blocks(dst, src, n):
    for q in range(3):
        m = pl.ds(aligned(jnp.minimum(3 * n + q, C // 128 - 1) * 128, 128), 128)
        dst[m, :] = src[:, m].T


def kernel(
    step_ref,
    mask_ref,
    gain_ref,
    bias_ref,
    latent_hbm,
    control_hbm,
    time_hbm,
    win_hbm,
    wout_hbm,
    cw_hbm,
    utemb_hbm,
    ctemb_hbm,
    zero_hbm,
    out_hbm,
    latent,
    control,
    time_w,
    win,
    wraw,
    craw,
    wt,
    ct,
    utemb,
    ctemb,
    zraw,
    zt,
    gathered,
    taps_sum,
    stack,
    wide,
    state,
    xf,
    norm_in,
    norm_cols,
    shifts,
    gate,
    masks,
    tv_mine,
    tv_all,
    tv_row,
    sib_send,
    sib_recv,
    far_send,
    far_recv,
    near_send,
    near_recv,
    out_buf,
    load_sem,
    zload_sem,
    za_send,
    za_recv,
    zb_send,
    zb_recv,
    out_sem,
    ag_send,
    ag_recv,
    d2d_send,
    d2d_recv,
    tv_send,
    tv_recv,
    sib_ssem,
    sib_rsem,
    rs_send,
    rs_recv,
):
    tensor = lax.axis_index("tensor")
    k = tensor // 2
    c = tensor % 2
    dp = lax.axis_index("dp")
    xi, yi, zi = dp // 8, (dp // 2) % 4, dp % 2
    k_up = (k + 1) % 4
    k_down = (k + 3) % 4
    k_far = (k + 2) % 4
    sib = {"tensor": k * 2 + (1 - c)}
    up = {"tensor": k_up * 2 + c}
    down = {"tensor": k_down * 2 + c}

    loads = {}
    for i, (name, src, dst) in enumerate(
        (
            ("latent", latent_hbm, latent),
            ("time", time_hbm, time_w),
            ("control", control_hbm, control),
            ("ctemb", ctemb_hbm, ctemb),
            ("utemb", utemb_hbm, utemb),
            ("craw", cw_hbm, craw.at[pl.ds(0, TAPS * CH), :]),
            ("win", win_hbm, win),
            ("wraw", wout_hbm, wraw.at[pl.ds(0, TAPS * CH), :]),
        )
    ):
        loads[name] = pltpu.make_async_copy(src, dst, load_sem.at[i])
        loads[name].start()
    zload = pltpu.make_async_copy(
        zero_hbm, zraw.at[pl.ds(aligned(k * CH, 32), CH), :], zload_sem
    )
    zload.start()

    barrier = pltpu.get_barrier_semaphore()

    def plane_peer(use_y, step):
        px = (xi + step * (1 - use_y)) % 4
        py = (yi + step * use_y) % 4
        return {"dp": (px * 4 + py) * 2 + zi}

    for step in range(1, SHARDS):
        pl.semaphore_signal(
            barrier, inc=1, device_id={"tensor": (tensor + step) % SHARDS}, device_id_type=MESH
        )
    for step in range(1, 4):
        for use_y in (0, 1):
            pl.semaphore_signal(
                barrier, inc=1, device_id=plane_peer(use_y, step), device_id_type=MESH
            )

    fill_masks(masks)
    norm_in[...] = jnp.zeros_like(norm_in)
    norm_in[0:3, 0:CH] = gain_ref[...]
    norm_in[3:6, 0:CH] = bias_ref[...]
    norm_cols[...] = norm_in[...].T

    loads["latent"].wait()

    def widen(src):
        def body(i, carry):
            r = aligned(i * 16, 16)
            xf[pl.ds(r, 16), :] = src[pl.ds(r, 16), :].astype(F32)
            return carry

        lax.fori_loop(0, CH // 16, body, 0)

    def slot_rows(shard, half):
        return pl.ds(aligned(32 * (shard % 4) + half * HALF, 16), HALF)

    def norm_half(which, half):
        for group in (2 * half, 2 * half + 1):
            rows = slice(group * GROUP, (group + 1) * GROUP)
            group_norm_silu(
                xf, norm_cols[rows, which : which + 1], norm_cols[rows, 3 + which : 4 + which], group
            )

    def piece(shard, half):
        return gathered.at[shard, slot_rows(shard, half), :]

    def remote(ref, send, recv, target, dst=None):
        return pltpu.make_async_remote_copy(
            src_ref=ref,
            dst_ref=ref if dst is None else dst,
            send_sem=send,
            recv_sem=recv,
            device_id=target,
            device_id_type=MESH,
        )

    def ag_copy(shard, half, slot, target):
        return remote(piece(shard, half), ag_send.at[slot], ag_recv.at[slot], target)

    def d2d_copy(shard, half, which):
        slot = which * 2 + half
        return remote(piece(shard, half), d2d_send.at[slot], d2d_recv.at[slot], sib)

    started = []

    def start(copy):
        copy.start()
        started.append(copy)

    def z_uses_y(r):
        return (0, 1, 1 - c, 0)[r]

    def z_index(r):
        return xi + z_uses_y(r) * (yi - xi)

    def z_rows(index, extra):
        if extra:
            return pl.ds(aligned(4 * 32 + 16 * index, 16), 16)
        return pl.ds(aligned(32 * index, 32), 32)

    def z_place(r, index, extra):
        offset = (128 + 16 * index) if extra else 32 * index
        return zraw.at[pl.ds(aligned(((k + r) % 4) * CH + offset, 16), 16 if extra else 32), :]

    def z_first(r, extra):
        index = z_index(r)
        return remote(
            zero_hbm.at[z_rows(index, extra), :],
            za_send.at[2 * r + extra],
            za_recv.at[2 * r + extra],
            {"tensor": ((k + 4 - r) % 4) * 2 + c},
            z_place(0, index, extra),
        )

    def z_second(r, step, index, extra):
        slot = (r * 4 + step) * 2 + extra
        return remote(
            z_place(r, index, extra),
            zb_send.at[slot],
            zb_recv.at[slot],
            plane_peer(z_uses_y(r), step),
        )

    def z_parts(index, act):
        act(0)

        @pl.when(index < 2)
        def _():
            act(1)

    pl.semaphore_wait(barrier, SHARDS - 1 + 6)
    for r in (1, 3, 2):
        z_parts(z_index(r), lambda extra: z_first(r, extra).start())

    def z_pass_on():
        for r in (1, 3, 2):
            index = z_index(r)

            def act(extra):
                z_first(r, extra).wait_send()
                z_first(r, extra).wait_recv()
                for step in range(1, 4):
                    z_second(r, step, index, extra).start()

            z_parts(index, act)

    def z_arrive():
        for r in (1, 3, 2):
            for step in range(1, 4):
                index = (z_index(r) + 4 - step) % 4
                z_parts(index, lambda extra: z_second(r, step, index, extra).wait_recv())
                z_parts(z_index(r), lambda extra: z_second(r, step, z_index(r), extra).wait_send())
        zload.wait()

    widen(latent)

    for half in (0, 1):
        norm_half(0, half)
        for i in range(HALF // 16):
            r = half * HALF + i * 16
            gathered[tensor, pl.ds(aligned(32 * (tensor % 4) + r, 16), 16), :] = xf[
                r : r + 16, :
            ].astype(BF16)
        if half == 0:
            start(ag_copy(tensor, 0, 0, up))
            start(d2d_copy(tensor, 0, 0))
        else:
            start(ag_copy(tensor, 1, 2, down))
            start(ag_copy(tensor, 1, 1, up))
            start(ag_copy(tensor, 0, 3, down))
            start(d2d_copy(tensor, 1, 0))

    loads["time"].wait()
    index = lax.broadcasted_iota(jnp.int32, (8, FREQ), 1)
    rates = jnp.exp(-math.log(10000.0) * (index % (FREQ // 2)).astype(F32) / (FREQ // 2))
    angles = step_ref[0].astype(F32) * rates
    rest = jnp.where(index < FREQ // 2, jnp.cos(angles), jnp.sin(angles))
    local = jnp.zeros((8, CH), F32)
    for _ in range(3):
        top = rest.astype(BF16)
        local = local + lax.dot_general(
            top, time_w[...], (((1,), (1,)), ((), ())), preferred_element_type=F32
        )
        rest = rest - top.astype(F32)
    tv_mine[...] = jnp.zeros_like(tv_mine)
    tv_mine[:, 0:CH] = silu(local)
    tv_mine[...] = pltpu.roll(tv_mine[...], 32 * (tensor % 4), 1)
    for step in range(1, SHARDS):
        start(
            remote(
                tv_mine,
                tv_send.at[step],
                tv_recv.at[step],
                {"tensor": (tensor + step) % SHARDS},
                tv_all.at[step],
            )
        )

    for shard in range(SHARDS):
        low = 32 * (shard % 4)
        if low:
            gathered[shard, 0:low, :] = jnp.zeros((low, CELLS), BF16)
        if low + CH < NB:
            gathered[shard, low + CH : NB, :] = jnp.zeros((NB - low - CH, CELLS), BF16)
    pad = KPAD - TAPS * CH
    stack[TAPS * CH : KPAD, :] = jnp.zeros((pad, CELLS), BF16)
    wraw[TAPS * CH : KPAD, :] = jnp.zeros((pad, C), BF16)
    craw[TAPS * CH : KPAD, :] = jnp.zeros((pad, C), BF16)

    tile = lax.broadcasted_iota(jnp.int32, (8, 128), 0)
    lane = lax.broadcasted_iota(jnp.int32, (8, 128), 1)
    spread = (lane % S // 4 == tile).astype(BF16)
    by_row = dot(mask_ref[0].astype(F32).astype(BF16), spread)
    for row in range(8):
        gate[:, row * 128 : (row + 1) * 128] = jnp.broadcast_to(by_row[row : row + 1, :], (8, 128))

    loads["control"].wait()
    widen(control)
    norm_half(2, 0)
    norm_half(2, 1)
    shifted_stack(xf, stack, masks)

    def window(shard):
        return pl.ds(aligned(128 * ((5 * shard) // 4), 128), NB)

    def conv_in(chip, first_time, dst=None, src=None):
        def body(n, carry):
            lanes = pl.ds(aligned(n * NB, NB), NB)
            total = dot(win[:, window(2 * chip)], gathered[2 * chip, :, lanes])
            total = total + dot(win[:, window(2 * chip + 1)], gathered[2 * chip + 1, :, lanes])
            if first_time:
                taps_sum[:, lanes] = total
            else:
                taps_sum[:, lanes] = taps_sum[:, lanes] + total
            if dst is not None:
                transpose_blocks(dst, src, n)
            return carry

        lax.fori_loop(0, NSTEPS, body, 0)

    loads["win"].wait()
    loads["craw"].wait()
    d2d_copy(tensor, 0, 0).wait_recv()
    d2d_copy(tensor, 1, 0).wait_recv()
    conv_in(k, True, ct, craw)
    z_pass_on()

    mate_k = lambda chip: chip * 2 + c
    other_k = lambda chip: chip * 2 + (1 - c)
    ag_copy(mate_k(k_down), 0, 0, up).wait_recv()
    start(ag_copy(mate_k(k_down), 0, 4, up))
    start(d2d_copy(mate_k(k_down), 0, 1))
    ag_copy(mate_k(k_up), 1, 2, down).wait_recv()
    start(ag_copy(mate_k(k_up), 1, 5, down))
    start(d2d_copy(mate_k(k_up), 1, 2))

    loads["wraw"].wait()

    def control_body(n, carry):
        lanes = pl.ds(aligned(n * NB, NB), NB)
        wide[:, lanes] = dot(ct[...], stack[:, lanes])
        transpose_blocks(wt, wraw, n)
        return carry

    lax.fori_loop(0, NSTEPS, control_body, 0)

    tv_row[...] = jnp.zeros_like(tv_row)
    tv_row[:, window(tensor)] = tv_row[:, window(tensor)] + tv_mine[...]
    for step in range(1, SHARDS):
        remote(tv_mine, tv_send.at[step], tv_recv.at[step], sib, tv_all.at[step]).wait_recv()
        owner = (tensor + SHARDS - step) % SHARDS
        tv_row[:, window(owner)] = tv_row[:, window(owner)] + tv_all[step]
    loads["ctemb"].wait()
    loads["utemb"].wait()
    for which, table in enumerate((utemb, ctemb)):

        def temb_body(i, carry):
            r = aligned(i * 16, 16)
            product = table[pl.ds(r, 16), :].astype(F32) * tv_row[0:1, :]
            shifts[which, pl.ds(r, 16), :] = jnp.broadcast_to(
                jnp.sum(product, axis=1, keepdims=True), (16, 128)
            )
            return carry

        lax.fori_loop(0, CH // 16, temb_body, 0)

    own = pl.ds(aligned(tensor * CH, 32), CH)
    wide[own, :] = wide[own, :] + (control[...].astype(F32) + shifts[1, :, 0:1])
    for d in range(4):
        theirs = pl.ds(aligned((2 * d + 1 - c) * CH, 32), CH)
        sib_send[d] = wide[theirs, :].astype(BF16)
        start(remote(sib_send.at[d], sib_ssem.at[d], sib_rsem.at[d], sib, sib_recv.at[d]))

    for d in range(4):
        mine = pl.ds(aligned((2 * d + c) * CH, 32), CH)
        remote(sib_send.at[d], sib_ssem.at[d], sib_rsem.at[d], sib, sib_recv.at[d]).wait_recv()
        state[pl.ds(d * CH, CH), :] = (wide[mine, :] + sib_recv[d].astype(F32)).astype(BF16)

    ag_copy(mate_k(k_down), 1, 1, up).wait_recv()
    start(d2d_copy(mate_k(k_down), 1, 1))
    ag_copy(mate_k(k_up), 0, 3, down).wait_recv()
    start(d2d_copy(mate_k(k_up), 0, 2))
    d2d_copy(other_k(k_down), 0, 1).wait_recv()
    d2d_copy(other_k(k_down), 1, 1).wait_recv()
    conv_in(k_down, False)
    d2d_copy(other_k(k_up), 1, 2).wait_recv()
    d2d_copy(other_k(k_up), 0, 2).wait_recv()
    z_arrive()
    conv_in(k_up, False, zt, zraw)
    ag_copy(mate_k(k_far), 0, 4, up).wait_recv()
    start(d2d_copy(mate_k(k_far), 0, 3))
    ag_copy(mate_k(k_far), 1, 5, down).wait_recv()
    start(d2d_copy(mate_k(k_far), 1, 3))
    d2d_copy(other_k(k_far), 0, 3).wait_recv()
    d2d_copy(other_k(k_far), 1, 3).wait_recv()
    conv_in(k_far, False)

    hrows = 32

    def hidden_body(i, carry):
        r = aligned(i * hrows, hrows)
        left, right, above, below = (
            jnp.concatenate([masks[m]] * (hrows // 8), 0) for m in range(4)
        )

        def tap(t):
            return taps_sum[pl.ds(aligned(t * CH + r, hrows), hrows), :]

        def row(dy):
            return (
                pltpu.roll(tap(3 * dy), 1, 1) * left
                + tap(3 * dy + 1)
                + pltpu.roll(tap(3 * dy + 2), CELLS - 1, 1) * right
            )

        total = pltpu.roll(row(0), S, 1) * above + row(1)
        total = total + pltpu.roll(row(2), CELLS - S, 1) * below
        total = total + shifts[0, pl.ds(r, hrows), 0:1]
        xf[pl.ds(r, hrows), :] = total.astype(BF16).astype(F32)
        return carry

    lax.fori_loop(0, CH // hrows, hidden_body, 0)
    norm_half(1, 0)
    norm_half(1, 1)
    shifted_stack(xf, stack, masks)

    for copy in started:
        copy.wait_send()

    def conv_out_rows(rows):
        def body(n, carry):
            lanes = pl.ds(aligned(n * NB, NB), NB)
            residual = dot(zt[rows, :], state[:, lanes]) * gate[0:1, lanes]
            wide[rows, lanes] = residual + dot(wt[rows, :], stack[:, lanes])
            return carry

        lax.fori_loop(0, NSTEPS, body, 0)

    def conv_out(chip):
        conv_out_rows(pl.ds(aligned(chip * 2 * CH, 64), 2 * CH))

    def to_sibling(slot, chip):
        theirs = pl.ds(aligned((2 * chip + 1 - c) * CH, 32), CH)
        sib_send[slot] = wide[theirs, :].astype(BF16)
        remote(
            sib_send.at[slot], sib_ssem.at[4 + slot], sib_rsem.at[4 + slot], sib, sib_recv.at[4 + slot]
        ).start()

    def from_sibling(slot):
        remote(
            sib_send.at[slot], sib_ssem.at[4 + slot], sib_rsem.at[4 + slot], sib, sib_recv.at[4 + slot]
        ).wait_recv()

    def own_sum(slot, chip, half):
        mine = pl.ds(aligned((2 * chip + c) * CH + half * HALF, 16), HALF)
        part = slice(half * HALF, (half + 1) * HALF)
        return wide[mine, :] + sib_recv[4 + slot, part, :].astype(F32)

    def far_copy(half):
        return remote(
            far_send.at[half], rs_send.at[half], rs_recv.at[half], (up, down)[half], far_recv.at[half]
        )

    def near_copy(way, half):
        slot = 2 + 2 * way + half
        return remote(
            near_send.at[way, half],
            rs_send.at[slot],
            rs_recv.at[slot],
            (up, down)[way],
            near_recv.at[way, half],
        )

    conv_out_rows(pl.ds(aligned(other_k(k_far) * CH, 32), CH))
    to_sibling(0, k_far)
    conv_out_rows(pl.ds(aligned(mate_k(k_far) * CH, 32), CH))
    conv_out(k_up)
    to_sibling(1, k_up)
    from_sibling(0)
    for half in (0, 1):
        far_send[half] = own_sum(0, k_far, half).astype(BF16)
        far_copy(half).start()
    conv_out(k_down)
    to_sibling(2, k_down)
    from_sibling(1)
    near_send[0, 1] = own_sum(1, k_up, 1).astype(BF16)
    near_copy(0, 1).start()
    conv_out(k)
    to_sibling(3, k)
    from_sibling(2)
    near_send[1, 0] = own_sum(2, k_down, 0).astype(BF16)
    near_copy(1, 0).start()
    from_sibling(3)
    far_copy(0).wait_recv()
    near_send[0, 0] = (own_sum(1, k_up, 0) + far_recv[0].astype(F32)).astype(BF16)
    near_copy(0, 0).start()
    far_copy(1).wait_recv()
    near_send[1, 1] = (own_sum(2, k_down, 1) + far_recv[1].astype(F32)).astype(BF16)
    near_copy(1, 1).start()
    for half in (0, 1):
        part = slice(half * HALF, (half + 1) * HALF)
        xf[part, :] = own_sum(3, k, half) + latent[part, :].astype(F32)
    near_copy(0, 1).wait_recv()
    xf[HALF:, :] = xf[HALF:, :] + near_recv[0, 1].astype(F32)
    near_copy(1, 0).wait_recv()
    xf[:HALF, :] = xf[:HALF, :] + near_recv[1, 0].astype(F32)
    near_copy(0, 0).wait_recv()
    out_buf[:HALF, :] = (xf[:HALF, :] + near_recv[0, 0].astype(F32)).astype(BF16)
    store0 = pltpu.make_async_copy(
        out_buf.at[pl.ds(0, HALF), :], out_hbm.at[pl.ds(0, HALF), :], out_sem.at[0]
    )
    store0.start()
    near_copy(1, 1).wait_recv()
    out_buf[HALF:, :] = (xf[HALF:, :] + near_recv[1, 1].astype(F32)).astype(BF16)
    store1 = pltpu.make_async_copy(
        out_buf.at[pl.ds(HALF, HALF), :], out_hbm.at[pl.ds(HALF, HALF), :], out_sem.at[1]
    )
    store1.start()
    for slot in range(4):
        remote(
            sib_send.at[slot], sib_ssem.at[4 + slot], sib_rsem.at[4 + slot], sib, sib_recv.at[4 + slot]
        ).wait_send()
    for half in (0, 1):
        far_copy(half).wait_send()
        near_copy(0, half).wait_send()
        near_copy(1, half).wait_send()
    store0.wait()
    store1.wait()


def local(
    latent_x,
    control_h,
    tile_mask,
    timestep,
    time_weight,
    norm_gain,
    norm_bias,
    unet_conv_in,
    unet_conv_out,
    control_conv,
    unet_temb,
    control_temb,
    zero_conv,
):
    flat = lambda w: w.reshape(TAPS * CH, C)
    smem = pl.BlockSpec(memory_space=pltpu.SMEM)
    vmem = pl.BlockSpec(memory_space=pltpu.VMEM)
    hbm = pl.BlockSpec(memory_space=pl.ANY)
    dma = pltpu.SemaphoreType.DMA
    return pl.pallas_call(
        kernel,
        out_shape=jax.ShapeDtypeStruct((CH, CELLS), BF16),
        in_specs=[smem, vmem, vmem, vmem] + [hbm] * 9,
        out_specs=hbm,
        scratch_shapes=[
            pltpu.VMEM((CH, CELLS), BF16),
            pltpu.VMEM((CH, CELLS), BF16),
            pltpu.VMEM((CH, FREQ), BF16),
            pltpu.VMEM((TAPS * CH, C), BF16),
            pltpu.VMEM((KPAD, C), BF16),
            pltpu.VMEM((KPAD, C), BF16),
            pltpu.VMEM((C, KPAD), BF16),
            pltpu.VMEM((C, KPAD), BF16),
            pltpu.VMEM((CH, C), BF16),
            pltpu.VMEM((CH, C), BF16),
            pltpu.VMEM((4 * CH, C), BF16),
            pltpu.VMEM((C, 4 * CH), BF16),
            pltpu.VMEM((SHARDS, NB, CELLS), BF16),
            pltpu.VMEM((TAPS * CH, CELLS), F32),
            pltpu.VMEM((KPAD, CELLS), BF16),
            pltpu.VMEM((C, CELLS), F32),
            pltpu.VMEM((4 * CH, CELLS), BF16),
            pltpu.VMEM((CH, CELLS), F32),
            pltpu.VMEM((8, 256), F32),
            pltpu.VMEM((256, 8), F32),
            pltpu.VMEM((2, CH, 128), F32),
            pltpu.VMEM((8, CELLS), F32),
            pltpu.VMEM((4, 8, CELLS), F32),
            pltpu.VMEM((8, NB), F32),
            pltpu.VMEM((SHARDS, 8, NB), F32),
            pltpu.VMEM((8, C), F32),
            pltpu.VMEM((4, CH, CELLS), BF16),
            pltpu.VMEM((8, CH, CELLS), BF16),
            pltpu.VMEM((2, HALF, CELLS), BF16),
            pltpu.VMEM((2, HALF, CELLS), BF16),
            pltpu.VMEM((2, 2, HALF, CELLS), BF16),
            pltpu.VMEM((2, 2, HALF, CELLS), BF16),
            pltpu.VMEM((CH, CELLS), BF16),
            dma((8,)),
            dma,
            dma((8,)),
            dma((8,)),
            dma((32,)),
            dma((32,)),
            dma((2,)),
            dma((6,)),
            dma((6,)),
            dma((8,)),
            dma((8,)),
            dma((8,)),
            dma((8,)),
            dma((8,)),
            dma((8,)),
            dma((6,)),
            dma((6,)),
        ],
        compiler_params=pltpu.CompilerParams(
            collective_id=0, has_side_effects=True, vmem_limit_bytes=62 * 1024 * 1024
        ),
        name="block",
    )(
        timestep,
        tile_mask,
        norm_gain,
        norm_bias,
        latent_x,
        control_h,
        time_weight.T,
        flat(unet_conv_in),
        flat(unet_conv_out),
        flat(control_conv),
        unet_temb,
        control_temb,
        zero_conv,
    )


def solution(mesh):
    placed = (
        P("tensor", "dp"),
        P("tensor", "dp"),
        P("dp", None, None),
        P("dp"),
        P(None, "tensor"),
        P(None, "tensor"),
        P(None, "tensor"),
        P(None, "tensor", None),
        P(None, "tensor", None),
        P(None, "tensor", None),
        P("tensor", None),
        P("tensor", None),
        P("tensor", None),
    )
    return jax.shard_map(
        local, mesh=mesh, in_specs=placed, out_specs=P("tensor", "dp"), check_vma=False
    )
```
